32 devices in a mesh: leaf: 4 (over z), panel: 8 (over y, x, core).
Axes of the slice: x: 2, y: 2, z: 4, core: 2. Of those that a mesh axis runs over, the one named last changes fastest.
Arguments:
- pix_grand: int32 [512, 8], P(None, 'leaf'), may hold values from 0 to 255
- pix_mid: int32 [512, 4], replicated, may hold values from 0 to 255
- pix_root: int32 [512], replicated, may hold values from 0 to 255
- parent: int32 [8], P('leaf'), may hold values from 0 to 3
- emit_grand: float32 [8, 4096, 256], P('leaf', 'panel'), may hold values from -232 to -1
- emit_mid: float32 [4, 4096, 256], P(None, 'panel'), may hold values from -232 to -1
- emit_root: float32 [4096, 256], P('leaf'), may hold values from -12 to -1
- weight_grand: float32 [8, 4096, 4096], P('leaf', None, 'panel'), may hold values from 2.4414063e-05 to 0.00048828125
- root_middle_weight: float32 [4, 4096, 4096], P(None, 'leaf', 'panel'), may hold values from 2.4414063e-05 to 0.00048828125
- prior: float32 [4096], P('leaf'), may hold values from 2.4414063e-05 to 0.00048828125
Outputs:
- loglik: float32 [512], replicated
- flow_grand: float32 [8, 4096, 4096], P('leaf', None, 'panel')
- flow_mid: float32 [4, 4096, 4096], P(None, 'leaf', 'panel')
The draws below stay inside these ranges and needn't reach their ends.
All inputs are finite; a program needn't handle non-finite values.
Results may differ from the reference program's by a relative error of at most 0.0003.
Values sent between devices are 32-bit elements; how exact they have to be, the bound alone decides.
A program may use at most 192 MiB of HBM per device.

```python
import math
import jax
import jax.numpy as jnp
from jax import lax

K = 4096
VALUES = 256
IMAGE_BATCH = 512
MID = 4
N_GRAND = 8
NODES = 13


def column_starts(key, count):
    perm_key, depth_key = jax.random.split(key, 2)
    row_keys = jax.random.split(perm_key, count)
    ranks = jax.vmap(lambda one_key: jax.random.permutation(one_key, VALUES))(row_keys)
    hits = max(1, VALUES // 16)
    chosen = ranks < hits
    depth = jax.random.uniform(depth_key, (count, VALUES), jnp.float32, 140.0, 220.0)
    return jnp.where(chosen, -depth, jnp.zeros_like(depth))


def coarse_partition(key, count):
    unit = jax.random.uniform(key, (count, K, VALUES), jnp.float32)
    return -1.0 - 11.0 * unit


def draw_emit_grand(key, part):
    base_key = jax.random.fold_in(key, 7101)
    coarse_random_key, offset_key = jax.random.split(base_key, 2)
    lookup_matrix = coarse_partition(coarse_random_key, N_GRAND) + column_starts(offset_key, N_GRAND)[:, None, :]
    return lookup_matrix.astype(jnp.float32)


def draw_emit_mid(key, part):
    base_key = jax.random.fold_in(key, 7202)
    coarse_random_key, offset_key = jax.random.split(base_key, 2)
    lookup_matrix = coarse_partition(coarse_random_key, MID) + column_starts(offset_key, MID)[:, None, :]
    return lookup_matrix.astype(jnp.float32)


def set_ends(drawn, rng, least, largest):
    longest = drawn.shape.index(max(drawn.shape))
    spots = []
    for shift in (0, 1):
        where = [jax.random.randint(jax.random.fold_in(rng, axis), (), 0, length) for axis, length in enumerate(drawn.shape)]
        where[longest] = (where[longest] + shift) % drawn.shape[longest]
        spots.append(tuple(where))
    return drawn.at[spots[0]].set(least).at[spots[1]].set(largest)


def block_levels(rng, dims, pieces, least, largest):
    level = 1.0
    for axis_at, parts in pieces:
        draws = jax.random.uniform(jax.random.fold_in(jax.random.fold_in(rng, 6), axis_at), (parts,), jnp.float32, least / len(pieces), largest / len(pieces))
        level = level * jnp.repeat(jnp.exp(draws), dims[axis_at] // parts).reshape((-1,) + (1,) * (len(dims) - 1 - axis_at))
    return level


def setup_inputs(seed: int = 0) -> dict:
    key_of = jax.random.split(jax.random.key(seed), 11)
    return {
        "pix_grand": set_ends(jax.random.randint(key_of[0], (IMAGE_BATCH, N_GRAND), 0, VALUES), jax.random.fold_in(key_of[0], 1), 0, VALUES - 1).astype(jnp.int32),
        "pix_mid": set_ends(jax.random.randint(key_of[1], (IMAGE_BATCH, MID), 0, VALUES), jax.random.fold_in(key_of[1], 1), 0, VALUES - 1).astype(jnp.int32),
        "pix_root": set_ends(jax.random.randint(key_of[2], (IMAGE_BATCH,), 0, VALUES), jax.random.fold_in(key_of[2], 1), 0, VALUES - 1).astype(jnp.int32),
        "parent": set_ends(jax.random.randint(key_of[3], (N_GRAND,), 0, MID), jax.random.fold_in(key_of[3], 1), 0, MID - 1).astype(jnp.int32),
        "emit_grand": draw_emit_grand(jax.random.fold_in(key_of[10], 71), 0),
        "emit_mid": draw_emit_mid(jax.random.fold_in(key_of[10], 71), 0),
        "emit_root": jnp.clip(-12.0 + 11.0 * jax.random.uniform(key_of[6], (K, VALUES), jnp.float32) ** block_levels(key_of[6], (K, VALUES), ((0, 4),), -0.2, 0.2), -12.0, -1.0),
        "weight_grand": jnp.clip(jnp.exp(math.log(0.00048828125) - 2.9957323 * jax.random.uniform(key_of[7], (N_GRAND, K, K), jnp.float32) ** block_levels(key_of[7], (N_GRAND, K, K), ((0, 4), (2, 8)), -0.2, 0.2)), 2.441406286379788e-05, 0.00048828125),
        "root_middle_weight": jnp.clip(jnp.exp(math.log(0.00048828125) - 2.9957323 * jax.random.uniform(key_of[8], (MID, K, K), jnp.float32) ** block_levels(key_of[8], (MID, K, K), ((1, 4), (2, 8)), -0.2, 0.2)), 2.441406286379788e-05, 0.00048828125),
        "prior": jnp.clip(jnp.exp(math.log(0.00048828125) - 2.9957323 * jax.random.uniform(key_of[9], (K,), jnp.float32) ** block_levels(key_of[9], (K,), ((0, 4),), -0.2, 0.2)), 2.441406286379788e-05, 0.00048828125),
    }


def reference(pix_grand, pix_mid, pix_root, parent, emit_grand, emit_mid, emit_root, weight_grand, root_middle_weight, prior):
    highest = lax.Precision.HIGHEST
    scale = (K * K) / IMAGE_BATCH

    def grand_up(index):
        lookup_matrix = emit_grand[index]
        potent = lookup_matrix[:, pix_grand[:, index]]
        upper = jnp.max(potent, axis=0)
        expo = jnp.exp(potent - upper[None, :])
        sums = jnp.dot(weight_grand[index], expo, precision=highest)
        return expo, sums, upper

    e_grand, grandchild_state_sum, top_grand = lax.map(grand_up, jnp.arange(N_GRAND, dtype=jnp.int32))
    m_grand = jnp.log(grandchild_state_sum) + top_grand[:, None, :]
    parent_hot = (parent[:, None] == jnp.arange(MID, dtype=jnp.int32)[None, :]).astype(jnp.float32)
    child_sum = jnp.einsum('gu,gkb->ukb', parent_hot, m_grand, precision=highest)
    a_mid = emit_mid[jnp.arange(MID, dtype=jnp.int32)[:, None, None], jnp.arange(K, dtype=jnp.int32)[None, :, None], jnp.transpose(pix_mid)[:, None, :]] + child_sum
    top_mid = jnp.max(a_mid, axis=1)
    e_mid = jnp.exp(a_mid - top_mid[:, None, :])
    s_mid = jnp.einsum('uij,ujb->uib', root_middle_weight, e_mid, precision=highest)
    m_mid = jnp.log(s_mid) + top_mid[:, None, :]
    scores = jnp.log(prior)[:, None] + emit_root[:, pix_root] + jnp.sum(m_mid, axis=0)
    top = jnp.max(scores, axis=0)
    expo_root = jnp.exp(scores - top[None, :])
    total = jnp.sum(expo_root, axis=0)
    loglik = (top + jnp.log(total)) / NODES
    q_root = expo_root / total[None, :]
    t_mid = q_root[None, :, :] / s_mid
    flow_mid = root_middle_weight * jnp.einsum('uib,ujb->uij', t_mid, e_mid, precision=highest) * scale
    q_mid = e_mid * jnp.einsum('uij,uib->ujb', root_middle_weight, t_mid, precision=highest)

    def grand_down(index):
        q_par = jnp.einsum('u,ukb->kb', parent_hot[index], q_mid, precision=highest)
        ratio = q_par / grandchild_state_sum[index]
        return weight_grand[index] * jnp.dot(ratio, jnp.transpose(e_grand[index]), precision=highest) * scale

    flow_grand = lax.map(grand_down, jnp.arange(N_GRAND, dtype=jnp.int32))
    return loglik, flow_grand, flow_mid
```

```python
import jax
import jax.numpy as jnp
from jax import lax
from jax.sharding import PartitionSpec as P

CHUNKS = 2


def one_hot(pixels, values):
    return (pixels[..., None, :] == jnp.arange(values, dtype=jnp.int32)[:, None]).astype(
        jnp.float32
    )


def lookup(lookup_matrix, pixels):
    return jnp.einsum(
        "ozd,odf->ozf",
        lookup_matrix,
        one_hot(jnp.transpose(pixels), lookup_matrix.shape[-1]),
        precision=lax.Precision.HIGHEST,
    )


def inward(total, axis, step):
    size = lax.axis_size(axis)
    if size % 2 or step >= size // 2 - 1:
        return total
    pairs = [(step, step + 1), (size - 1 - step, size - 2 - step)]
    return total + lax.ppermute(total, axis, pairs)


def across(total, axis):
    size = lax.axis_size(axis)
    if size % 2:
        return lax.psum(total, axis)
    half = size // 2
    for step in range(1, half - 1):
        total = inward(total, axis, step)
    return total + lax.ppermute(total, axis, [(half - 1, half), (half, half - 1)])


def outward(total, axis):
    size = lax.axis_size(axis)
    if size % 2:
        return total
    me = lax.axis_index(axis)
    for source in range(size // 2 - 1, 0, -1):
        pairs = [(source, source - 1), (size - 1 - source, size - source)]
        received = lax.ppermute(total, axis, pairs)
        total = jnp.where((me == source - 1) | (me == size - source), received, total)
    return total


def shards(
    pix_grand,
    pix_mid,
    pix_root,
    parent,
    emit_grand,
    emit_mid,
    emit_root,
    weight_grand,
    root_middle_weight,
    prior,
):
    high = lax.Precision.HIGH
    highest = lax.Precision.HIGHEST
    images = pix_grand.shape[0]
    states = weight_grand.shape[1]
    groups = parent.shape[0]
    middles = root_middle_weight.shape[0]
    leaves, panels = lax.axis_size("leaf"), lax.axis_size("panel")
    my_leaf, my_panel = lax.axis_index("leaf"), lax.axis_index("panel")
    scale = states * states / images
    nodes = groups * leaves + middles + 1
    width = images // CHUNKS
    rows = emit_root.shape[0] // panels

    a_grand = lookup(emit_grand, pix_grand)
    grand_upper = jnp.max(lax.all_gather(jnp.max(a_grand, axis=1), "panel"), axis=0)
    a_mid_own = lookup(emit_mid, pix_mid)
    e_grand = jnp.exp(a_grand - grand_upper[:, None, :])
    own_emit = lax.dynamic_slice_in_dim(emit_root, my_panel * rows, rows, 0)
    own_prior = lax.dynamic_slice_in_dim(prior, my_panel * rows, rows, 0)
    root_own = jnp.log(own_prior)[:, None] + jnp.dot(
        own_emit, one_hot(pix_root, emit_root.shape[1]), precision=highest
    )

    spans = [slice(chunk * width, (chunk + 1) * width) for chunk in range(CHUNKS)]
    s_all = [
        [
            lax.psum_scatter(
                jnp.dot(weight_grand[g], e_grand[g, :, here], precision=high),
                "panel",
                scatter_dimension=0,
                tiled=True,
            )
            for g in range(groups)
        ]
        for here in spans
    ]

    def children(s_own, here):
        m_own = [jnp.log(s_own[g]) + grand_upper[g, None, here] for g in range(groups)]
        return [
            inward(sum(jnp.where(parent[g] == u, m_own[g], 0.0) for g in range(groups)), "leaf", 0)
            for u in range(middles)
        ]

    logliks, mid_flows, grand_flows = [], [], []
    child = [outward(across(begun, "leaf"), "leaf") for begun in children(s_all[0], spans[0])]
    ratio_before, q_begun = None, []

    def divided(begun, chunk):
        q_mid = [outward(value, "leaf") for value in begun]
        return jnp.stack(
            [
                sum(jnp.where(parent[g] == u, q_mid[u], 0.0) for u in range(middles))
                / s_all[chunk][g]
                for g in range(groups)
            ],
            axis=1,
        )

    def collect(ratio_own, here):
        t_grand = lax.all_gather(ratio_own, "panel", axis=0, tiled=True)
        grand_flows.append(
            jnp.einsum("igb,gjb->gij", t_grand, e_grand[:, :, here], precision=high)
        )

    for chunk, here in enumerate(spans):
        a_mid = jnp.stack([a_mid_own[u, :, here] + child[u] for u in range(middles)])
        mid_local = jnp.max(a_mid, axis=1)
        e_local = jnp.exp(a_mid - mid_local[:, None, :])
        partial = jnp.einsum("uij,ujb->iub", root_middle_weight, e_local, precision=high)
        mid_upper = jnp.max(lax.all_gather(mid_local, "panel"), axis=0)
        begun = []
        if chunk + 1 < CHUNKS:
            s_all[chunk + 1], mid_local = lax.optimization_barrier((s_all[chunk + 1], mid_local))
            begun = children(s_all[chunk + 1], spans[chunk + 1])
        partial, begun[:1], q_begun[:1] = lax.optimization_barrier(
            (partial, begun[:1], q_begun[:1])
        )
        begun = [across(value, "leaf") for value in begun]
        q_begun = [across(value, "leaf") for value in q_begun]
        shift = jnp.exp(mid_local - mid_upper)
        e_mid = e_local * shift[:, None, :]
        s_mid = lax.psum_scatter(
            partial * shift[None], "panel", scatter_dimension=0, tiled=True
        )
        s_mid, begun, q_begun = lax.optimization_barrier((s_mid, begun, q_begun))
        child = [outward(value, "leaf") for value in begun]
        ratio_before = divided(q_begun, chunk - 1) if chunk else None
        scores = root_own[:, here] + jnp.sum(jnp.log(s_mid) + mid_upper[None], axis=1)
        root_local = jnp.max(scores, axis=0)
        expo_root = jnp.exp(scores - root_local[None, :])
        stats = lax.all_gather(
            jnp.stack([root_local, jnp.sum(expo_root, axis=0)]), ("leaf", "panel")
        )
        t_rows = lax.all_gather(expo_root[:, None, :] / s_mid, "panel", axis=0)
        if ratio_before is not None:
            t_rows, ratio_before = lax.optimization_barrier((t_rows, ratio_before))
            collect(ratio_before, spans[chunk - 1])
        upper = jnp.max(stats[:, 0], axis=0)
        total = jnp.sum(stats[:, 1] * jnp.exp(stats[:, 0] - upper[None]), axis=0)
        logliks.append((upper + jnp.log(total)) / nodes)
        block = lax.dynamic_slice_in_dim(stats[:, 0], my_leaf * panels, panels, 0)
        share = jnp.exp(block - upper[None]) / total[None]
        t_mid = (t_rows * share[:, None, None, :]).reshape(panels * rows, middles, width)
        q_part = e_mid * jnp.einsum("uij,iub->ujb", root_middle_weight, t_mid, precision=high)
        if chunk + 1 < CHUNKS:
            child, q_part = lax.optimization_barrier((child, q_part))
        q_begun = [inward(q_part[u], "leaf", 0) for u in range(middles)]
        mid_flows.append(jnp.einsum("iub,ujb->uij", t_mid, e_mid, precision=high))
    q_begun = [across(value, "leaf") for value in q_begun]
    collect(divided(q_begun, CHUNKS - 1), spans[-1])
    return (
        jnp.concatenate(logliks),
        weight_grand * sum(grand_flows) * scale,
        root_middle_weight * sum(mid_flows) * scale,
    )


def solution(mesh):
    placed = (
        P(None, "leaf"),
        P(),
        P(),
        P("leaf"),
        P("leaf", "panel", None),
        P(None, "panel", None),
        P("leaf", None),
        P("leaf", None, "panel"),
        P(None, "leaf", "panel"),
        P("leaf"),
    )
    return jax.shard_map(
        shards,
        mesh=mesh,
        in_specs=placed,
        out_specs=(P(), P("leaf", None, "panel"), P(None, "leaf", "panel")),
        check_vma=False,
    )
```

```python
import jax
import jax.numpy as jnp
from jax import lax
from jax.sharding import PartitionSpec as P

CHUNKS = 1


def one_hot(pixels, values):
    return (pixels[..., None, :] == jnp.arange(values, dtype=jnp.int32)[:, None]).astype(
        jnp.float32
    )


def lookup(lookup_matrix, pixels):
    return jnp.einsum(
        "ozd,odf->ozf",
        lookup_matrix,
        one_hot(jnp.transpose(pixels), lookup_matrix.shape[-1]),
        precision=lax.Precision.HIGHEST,
    )


def inward(total, axis, step):
    size = lax.axis_size(axis)
    if size % 2 or step >= size // 2 - 1:
        return total
    pairs = [(step, step + 1), (size - 1 - step, size - 2 - step)]
    return total + lax.ppermute(total, axis, pairs)


def across(total, axis):
    size = lax.axis_size(axis)
    if size % 2:
        return lax.psum(total, axis)
    half = size // 2
    for step in range(1, half - 1):
        total = inward(total, axis, step)
    return total + lax.ppermute(total, axis, [(half - 1, half), (half, half - 1)])


def outward(total, axis):
    size = lax.axis_size(axis)
    if size % 2:
        return total
    me = lax.axis_index(axis)
    for source in range(size // 2 - 1, 0, -1):
        pairs = [(source, source - 1), (size - 1 - source, size - source)]
        received = lax.ppermute(total, axis, pairs)
        total = jnp.where((me == source - 1) | (me == size - source), received, total)
    return total


def shards(
    pix_grand,
    pix_mid,
    pix_root,
    parent,
    emit_grand,
    emit_mid,
    emit_root,
    weight_grand,
    root_middle_weight,
    prior,
):
    high = lax.Precision.HIGH
    highest = lax.Precision.HIGHEST
    images = pix_grand.shape[0]
    states = weight_grand.shape[1]
    groups = parent.shape[0]
    middles = root_middle_weight.shape[0]
    leaves, panels = lax.axis_size("leaf"), lax.axis_size("panel")
    my_leaf, my_panel = lax.axis_index("leaf"), lax.axis_index("panel")
    scale = states * states / images
    nodes = groups * leaves + middles + 1
    width = images // CHUNKS
    rows = emit_root.shape[0] // panels

    a_grand = lookup(emit_grand, pix_grand)
    grand_upper = jnp.max(lax.all_gather(jnp.max(a_grand, axis=1), "panel"), axis=0)
    a_mid_own = lookup(emit_mid, pix_mid)
    e_grand = jnp.exp(a_grand - grand_upper[:, None, :])
    own_emit = lax.dynamic_slice_in_dim(emit_root, my_panel * rows, rows, 0)
    own_prior = lax.dynamic_slice_in_dim(prior, my_panel * rows, rows, 0)
    root_own = jnp.log(own_prior)[:, None] + jnp.dot(
        own_emit, one_hot(pix_root, emit_root.shape[1]), precision=highest
    )

    spans = [slice(chunk * width, (chunk + 1) * width) for chunk in range(CHUNKS)]
    s_all = [
        [
            lax.psum_scatter(
                jnp.dot(weight_grand[g], e_grand[g, :, here], precision=high),
                "panel",
                scatter_dimension=0,
                tiled=True,
            )
            for g in range(groups)
        ]
        for here in spans
    ]

    def children(s_own, here):
        m_own = [jnp.log(s_own[g]) + grand_upper[g, None, here] for g in range(groups)]
        return [
            inward(sum(jnp.where(parent[g] == u, m_own[g], 0.0) for g in range(groups)), "leaf", 0)
            for u in range(middles)
        ]

    logliks, mid_flows, grand_flows = [], [], []
    child = [outward(across(begun, "leaf"), "leaf") for begun in children(s_all[0], spans[0])]
    ratio_before, q_begun = None, []

    def divided(begun, chunk):
        q_mid = [outward(value, "leaf") for value in begun]
        return jnp.stack(
            [
                sum(jnp.where(parent[g] == u, q_mid[u], 0.0) for u in range(middles))
                / s_all[chunk][g]
                for g in range(groups)
            ],
            axis=1,
        )

    def collect(ratio_own, here):
        t_grand = lax.all_gather(ratio_own, "panel", axis=0, tiled=True)
        grand_flows.append(
            jnp.einsum("igb,gjb->gij", t_grand, e_grand[:, :, here], precision=high)
        )

    for chunk, here in enumerate(spans):
        a_mid = jnp.stack([a_mid_own[u, :, here] + child[u] for u in range(middles)])
        mid_local = jnp.max(a_mid, axis=1)
        e_local = jnp.exp(a_mid - mid_local[:, None, :])
        partial = jnp.einsum("uij,ujb->iub", root_middle_weight, e_local, precision=high)
        mid_upper = jnp.max(lax.all_gather(mid_local, "panel"), axis=0)
        begun = []
        if chunk + 1 < CHUNKS:
            s_all[chunk + 1], mid_local = lax.optimization_barrier((s_all[chunk + 1], mid_local))
            begun = children(s_all[chunk + 1], spans[chunk + 1])
        partial, begun[:1], q_begun[:1] = lax.optimization_barrier(
            (partial, begun[:1], q_begun[:1])
        )
        begun = [across(value, "leaf") for value in begun]
        q_begun = [across(value, "leaf") for value in q_begun]
        shift = jnp.exp(mid_local - mid_upper)
        e_mid = e_local * shift[:, None, :]
        s_mid = lax.psum_scatter(
            partial * shift[None], "panel", scatter_dimension=0, tiled=True
        )
        s_mid, begun, q_begun = lax.optimization_barrier((s_mid, begun, q_begun))
        child = [outward(value, "leaf") for value in begun]
        ratio_before = divided(q_begun, chunk - 1) if chunk else None
        scores = root_own[:, here] + jnp.sum(jnp.log(s_mid) + mid_upper[None], axis=1)
        root_local = jnp.max(scores, axis=0)
        expo_root = jnp.exp(scores - root_local[None, :])
        stats = lax.all_gather(
            jnp.stack([root_local, jnp.sum(expo_root, axis=0)]), ("leaf", "panel")
        )
        t_rows = lax.all_gather(expo_root[:, None, :] / s_mid, "panel", axis=0)
        if ratio_before is not None:
            t_rows, ratio_before = lax.optimization_barrier((t_rows, ratio_before))
            collect(ratio_before, spans[chunk - 1])
        upper = jnp.max(stats[:, 0], axis=0)
        total = jnp.sum(stats[:, 1] * jnp.exp(stats[:, 0] - upper[None]), axis=0)
        logliks.append((upper + jnp.log(total)) / nodes)
        block = lax.dynamic_slice_in_dim(stats[:, 0], my_leaf * panels, panels, 0)
        share = jnp.exp(block - upper[None]) / total[None]
        t_mid = (t_rows * share[:, None, None, :]).reshape(panels * rows, middles, width)
        q_part = e_mid * jnp.einsum("uij,iub->ujb", root_middle_weight, t_mid, precision=high)
        if chunk + 1 < CHUNKS:
            child, q_part = lax.optimization_barrier((child, q_part))
        q_begun = [inward(q_part[u], "leaf", 0) for u in range(middles)]
        mid_flows.append(jnp.einsum("iub,ujb->uij", t_mid, e_mid, precision=high))
    q_begun = [across(value, "leaf") for value in q_begun]
    collect(divided(q_begun, CHUNKS - 1), spans[-1])
    return (
        jnp.concatenate(logliks),
        weight_grand * sum(grand_flows) * scale,
        root_middle_weight * sum(mid_flows) * scale,
    )


def solution(mesh):
    placed = (
        P(None, "leaf"),
        P(),
        P(),
        P("leaf"),
        P("leaf", "panel", None),
        P(None, "panel", None),
        P("leaf", None),
        P("leaf", None, "panel"),
        P(None, "leaf", "panel"),
        P("leaf"),
    )
    return jax.shard_map(
        shards,
        mesh=mesh,
        in_specs=placed,
        out_specs=(P(), P("leaf", None, "panel"), P(None, "leaf", "panel")),
        check_vma=False,
    )
```
